128 devices in a mesh: ia: 8 (over z_lo, x), ja: 16 (over z_hi, y, core).
Axes of the slice: x: 4, y: 4, z: 4 (z_hi: 2, z_lo: 2; z = z_hi * 2 + z_lo), core: 2. Of those that a mesh axis runs over, the one named last changes fastest.
Arguments:
- tensor: float32 [8, 8192, 8192], P(None, 'ia', 'ja'), may hold values from -6 to 6
- b_init: float32 [8192, 64], P('ja'), may hold values from -0.0625 to 0.0625
- c_init: float32 [8, 64], replicated, may hold values from -6 to 6
Outputs:
- factor_a: float32 [8192, 64], P(('ia', 'ja'))
- factor_b: float32 [8192, 64], P('ja')
- factor_c: float32 [8, 64], replicated
The draws below stay inside these ranges and needn't reach their ends.
All inputs are finite; a program needn't handle non-finite values.
Results may differ from the reference program's by a relative error of at most 0.0003.
Values sent between devices are 32-bit elements; how exact they have to be, the bound alone decides.
A program may use at most 128 MiB of HBM per device.

```python
import jax
import jax.numpy as jnp
from jax import lax

I = 8192
J = 8192
K = 8
R = 64
SWEEPS = 4


def steps_of(own_key, extent, shards, least, top_value):
    def one(position, blocks):
        heights = jax.random.uniform(jax.random.fold_in(jax.random.fold_in(own_key, 6), position), (blocks,), jnp.float32, least / len(shards), top_value / len(shards))
        return jnp.repeat(jnp.exp(heights), extent[position] // blocks).reshape((-1,) + (1,) * (len(extent) - position - 1))

    level = one(*shards[0])
    for cut in shards[1:]:
        level = level * one(*cut)
    return level


def centred(key, dims, deviation, limit, pieces=(), dtype=jnp.bfloat16):
    values = deviation * jax.random.normal(key, dims, jnp.float32)
    if pieces:
        values = values * steps_of(key, dims, pieces, -0.22, 0.18)
    return jnp.clip(values, -limit, limit).astype(dtype)


def setup_inputs(seed: int = 0) -> dict:
    key_list = jax.random.split(jax.random.key(seed), 4)
    tensor = centred(key_list[0], (K, I, J), 1.0, 6.0, ((1, 8), (2, 16)), jnp.float32)
    b_init = centred(key_list[1], (J, R), J ** -0.5, 0.0625, ((0, 16),), jnp.float32)
    c_init = centred(key_list[2], (K, R), 1.0, 6.0, (), jnp.float32)
    return dict(tensor=tensor, b_init=b_init, c_init=c_init)


HIGH = lax.Precision.HIGHEST

def gram_of(factor):
    return jnp.dot(factor.T.astype(jnp.float32), factor.astype(jnp.float32), precision=HIGH, preferred_element_type=jnp.float32)

def solve_rows(products, normal):
    lower = jnp.linalg.cholesky(normal)
    return jax.scipy.linalg.cho_solve((lower, True), products.T).T

def unit_columns(factor, raw):
    norms = jnp.sqrt(jnp.diagonal(raw) + 1e-06)
    return (factor / norms[None, :], raw / (norms[:, None] * norms[None, :]))

def reference(tensor, b_init, c_init):
    factor_b = b_init
    factor_c = c_init
    gram_b = gram_of(factor_b)
    gram_c = gram_of(factor_c)
    factor_a = None
    for sweep in range(SWEEPS):
        partial_value = jnp.einsum('kij,jr->kir', tensor, factor_b, precision=HIGH)
        mode_one = jnp.einsum('kir,kr->ir', partial_value, factor_c, precision=HIGH)
        factor_a = solve_rows(mode_one, gram_b * gram_c)
        factor_a, gram_a = unit_columns(factor_a, gram_of(factor_a))
        partial_value = jnp.einsum('kij,ir->kjr', tensor, factor_a, precision=HIGH)
        mode_two = jnp.einsum('kjr,kr->jr', partial_value, factor_c, precision=HIGH)
        factor_b = solve_rows(mode_two, gram_a * gram_c)
        factor_b, gram_b = unit_columns(factor_b, gram_of(factor_b))
        partial_value = jnp.einsum('kij,jr->kir', tensor, factor_b, precision=HIGH)
        mode_three = jnp.einsum('kir,ir->kr', partial_value, factor_a, precision=HIGH)
        factor_c = solve_rows(mode_three, gram_a * gram_b)
        gram_c = gram_of(factor_c)
    return (factor_a, factor_b, factor_c)
```

```python
import functools

import jax
import jax.numpy as jnp
from jax import lax
from jax.experimental import pallas as pl
from jax.experimental.pallas import tpu as pltpu
from jax.sharding import PartitionSpec as P

SWEEPS = 4
K = 8
R = 64
NI = 8
NJ = 16
ROWS = 1024
COLS = 512
HIGH = lax.Precision.HIGHEST
F32 = jnp.float32
BF16 = jnp.bfloat16
MESH = pl.DeviceIdType.MESH


def dot(a, b, ca, cb, precision=None):
    return lax.dot_general(
        a, b, (((ca,), (cb,)), ((), ())), precision=precision, preferred_element_type=F32
    )


def split(x):
    high = x.astype(BF16)
    return high, (x - high.astype(F32)).astype(BF16)


def inverse(a, b=8):
    m = 8
    lane = lax.broadcasted_iota(jnp.int32, (m, R), 1)
    sub = lax.broadcasted_iota(jnp.int32, (m, R), 0)
    t = [a[8 * i : 8 * i + 8] for i in range(8)]

    def rep(v):
        return jnp.broadcast_to(v, (m, R))

    for k0 in range(0, R, b):
        kt, ks = k0 // 8, k0 % 8
        cols = [[rep(t[i][:, k0 + j : k0 + j + 1]) for i in range(8)] for j in range(b)]
        rows = [rep(t[kt][ks + j : ks + j + 1, :]) for j in range(b)]
        piv = [[rep(cols[j][kt][ks + i : ks + i + 1, :]) for j in range(b)] for i in range(b)]
        inside = (lane >= k0) & (lane < k0 + b)
        rows = [jnp.where(inside, jnp.where(lane == k0 + i, 1.0, 0.0), rows[i]) for i in range(b)]
        for i in range(b):
            p = 1.0 / piv[i][i]
            rows[i] = rows[i] * p
            for j in range(i + 1, b):
                piv[i][j] = piv[i][j] * p
            for r in range(b):
                if r != i:
                    f = piv[r][i]
                    for j in range(i + 1, b):
                        piv[r][j] = piv[r][j] - f * piv[i][j]
                    rows[r] = rows[r] - f * rows[i]
        for i in range(8):
            x = jnp.where(inside, 0.0, t[i])
            for j in range(b):
                x = x - cols[j][i] * rows[j]
            t[i] = x
        for j in range(b):
            t[kt] = jnp.where(sub == ks + j, rows[j], t[kt])
    return jnp.concatenate(t, axis=0)


def pack(gram):
    wide = jnp.concatenate([gram, jnp.zeros((R, 128 - R), F32)], axis=1)
    return wide[:32] + pltpu.roll(wide[32:], 64, 1)


def unpack(x):
    return jnp.concatenate([x[:, :R], pltpu.roll(x, 64, 1)[:, :R]], axis=0)


def diagonal(gram):
    same = lax.broadcasted_iota(jnp.int32, (R, R), 0) == lax.broadcasted_iota(jnp.int32, (R, R), 1)
    only = jnp.where(same, gram, 0.0)
    return jnp.sum(only, axis=0, keepdims=True), jnp.sum(only, axis=1, keepdims=True)


def unit(raw):
    row, col = diagonal(raw)
    row, col = jnp.sqrt(row + 1e-6), jnp.sqrt(col + 1e-6)
    return raw / (col * row), 1.0 / row, 1.0 / col


def turned(x):
    return jnp.concatenate([x, jnp.zeros_like(x)], axis=0).T


class Exchange:
    def __init__(self, axis, n, source, target, send, recv):
        me = lax.axis_index(axis)
        self.copies = []
        for d in range(1, n):
            peer = lax.rem(me + d, n)
            self.copies.append(
                pltpu.make_async_remote_copy(
                    src_ref=source(peer),
                    dst_ref=target(d),
                    send_sem=send.at[d],
                    recv_sem=recv.at[d],
                    device_id={axis: peer},
                    device_id_type=MESH,
                )
            )

    def start(self):
        for copy in self.copies:
            copy.start()

    def wait_recv(self):
        for copy in self.copies:
            copy.wait_recv()

    def wait_send(self):
        for copy in self.copies:
            copy.wait_send()


def kernel(
    t_hbm, b0, c0, out_a, out_b, out_c,
    stage, t16, prod, q_ref, w1, w2, at, bt, crow, ccol, gram_b, gram_c, scale_a, tmp,
    s1, r1, g1, s2, r2, g2, ga, gb, m3a, m3b,
    load_sem, s1s, s1r, g1s, g1r, s2s, s2r, g2s, g2r, gas, gar, gbs, gbr, mas, mar, mbs, mbr,
):
    me_i, me_j = lax.axis_index("ia"), lax.axis_index("ja")

    def load(k, slot):
        return pltpu.make_async_copy(t_hbm.at[k], stage.at[slot], load_sem.at[slot])

    load(0, 0).start()
    load(1, 1).start()

    barrier = pltpu.get_barrier_semaphore()
    for d in range(1, NJ):
        pl.semaphore_signal(barrier, inc=1, device_id={"ja": lax.rem(me_j + d, NJ)}, device_id_type=MESH)
    for d in range(1, NI):
        pl.semaphore_signal(barrier, inc=1, device_id={"ia": lax.rem(me_i + d, NI)}, device_id_type=MESH)
    pl.semaphore_wait(barrier, NJ - 1 + NI - 1)

    scatter1 = Exchange("ja", NJ, lambda p: s1.at[p], lambda d: r1.at[d], s1s, s1r)
    gather1 = Exchange("ja", NJ, lambda p: g1.at[me_j], lambda d: g1.at[me_j], g1s, g1r)
    scatter2 = Exchange("ia", NI, lambda p: s2.at[p], lambda d: r2.at[d], s2s, s2r)
    gather2 = Exchange("ia", NI, lambda p: g2.at[me_i], lambda d: g2.at[me_i], g2s, g2r)
    share_ga = Exchange("ia", NI, lambda p: ga.at[me_i], lambda d: ga.at[me_i], gas, gar)
    share_gb = Exchange("ja", NJ, lambda p: gb.at[me_j], lambda d: gb.at[me_j], gbs, gbr)
    share_ma = Exchange("ia", NI, lambda p: m3a.at[me_i], lambda d: m3a.at[me_i], mas, mar)
    share_mb = Exchange("ja", NJ, lambda p: m3b.at[me_j], lambda d: m3b.at[me_j], mbs, mbr)

    def total(ref, n):
        x = ref[0]
        for i in range(1, n):
            x = x + ref[i]
        return x

    def set_w1(b_t):
        high = b_t.astype(BF16).astype(F32)
        both = jnp.concatenate([high, b_t - high], axis=0).T
        w1[:COLS] = both.astype(BF16)
        keep = lax.broadcasted_iota(jnp.int32, (COLS, 128), 1) < R
        w1[COLS:] = jnp.where(keep, both, 0.0).astype(BF16)

    def products_b(k, _):
        prod[k] = dot(t16[k], w1[...], 1, 0)
        return 0

    def set_c(c, inv_norm):
        scaled = c * inv_norm
        crow[...] = jnp.concatenate([scaled, scaled], axis=1)
        wide = jnp.concatenate([c, jnp.zeros((K, 128 - R), F32)], axis=1)
        c_t = jnp.concatenate([wide, jnp.zeros((128 - K, 128), F32)], axis=0).T[:R]
        for k in range(K):
            ccol[k] = jnp.broadcast_to(c_t[:, k : k + 1], (R, 128))
        gram_c[...] = dot(c_t, c_t, 1, 1, HIGH)

    b_t = jnp.concatenate([b0[...], jnp.zeros((COLS, 128 - R), F32)], axis=1).T[:R]
    gb[me_j] = pack(dot(b_t, b_t, 1, 1, HIGH))
    share_gb.start()
    set_w1(b_t)
    set_c(c0[...], jnp.ones((1, R), F32))

    def first(k, _):
        slot = lax.rem(k, 2)
        load(k, slot).wait()
        high, low = split(stage[slot])
        t16[k, :, :COLS] = high
        t16[k, :, COLS:] = low

        @pl.when(k + 2 < K)
        def _():
            load(k + 2, slot).start()

        return products_b(k, 0)

    lax.fori_loop(0, K, first, 0)
    share_gb.wait_recv()
    gram_b[...] = unpack(total(gb, NJ))
    share_gb.wait_send()

    def sweep(s, _):
        for q in range(8):
            rows = pl.ds(128 * q, 128)
            acc = prod[0, rows, :] * crow[0:1]
            for k in range(1, K):
                acc = acc + prod[k, rows, :] * crow[k : k + 1]
            acc = acc.T
            acc = acc[:R] + acc[R:]
            s1[2 * q] = acc[:32]
            s1[2 * q + 1] = acc[32:]
        scatter1.start()
        solve_a = inverse(gram_b[...] * gram_c[...])
        scatter1.wait_recv()
        acc = s1[me_j]
        for d in range(1, NJ):
            acc = acc + r1[d]
        g1[me_j] = acc
        gather1.start()
        gather1.wait_recv()
        for q in range(8):
            block = jnp.concatenate([g1[2 * q], g1[2 * q + 1]], axis=0)
            block = dot(solve_a, block, 1, 0, HIGH)
            at[q] = block
            high, low = split(block)
            w2[:R, 128 * q : 128 * q + 128] = high
            w2[R:, 128 * q : 128 * q + 128] = low
        a_t = jnp.concatenate([at[q] for q in range(8)], axis=1)
        ga[me_i] = pack(dot(a_t, a_t, 1, 1, HIGH))
        share_ga.start()

        def products_a(k, acc):
            x = dot(w2[...], t16[k], 1, 0)
            x = x[:R, :COLS] + x[R:, :COLS] + x[:R, COLS:]
            q_ref[k] = x
            c = ccol[k]
            return acc + x * jnp.concatenate([c] * 4, axis=1)

        acc = lax.fori_loop(0, K, products_a, jnp.zeros((R, COLS), F32))
        for j in range(4):
            s2[2 * j] = acc[:32, 128 * j : 128 * j + 128]
            s2[2 * j + 1] = acc[32:, 128 * j : 128 * j + 128]
        scatter2.start()
        share_ga.wait_recv()
        gram_a, row_a, col_a = unit(unpack(total(ga, NI)))
        scale_a[...] = jnp.broadcast_to(col_a, (R, 128))
        solve_b = inverse(gram_a * gram_c[...]) * row_a
        scatter2.wait_recv()
        acc = s2[me_i]
        for d in range(1, NI):
            acc = acc + r2[d]
        g2[me_i] = acc
        gather2.start()
        gather2.wait_recv()
        acc = jnp.concatenate(
            [jnp.concatenate([g2[2 * j], g2[2 * j + 1]], axis=0) for j in range(4)], axis=1
        )
        b_t = dot(solve_b, acc, 1, 0, HIGH)
        bt[...] = b_t

        scaled = b_t * col_a
        lane = lax.broadcasted_iota(jnp.int32, (R, 128), 1)
        sums = jnp.zeros((R, 128), F32)
        for k in range(K):
            x = q_ref[k] * scaled
            x = x[:, :128] + x[:, 128:256] + x[:, 256:384] + x[:, 384:]
            sums = jnp.where(lane == k, jnp.sum(x, axis=1, keepdims=True), sums)
        m3a[me_i] = turned(sums)[:K]
        share_ma.start()
        gb[me_j] = pack(dot(b_t, b_t, 1, 1, HIGH))
        share_gb.start()

        @pl.when(s < SWEEPS - 1)
        def _():
            set_w1(b_t)
            lax.fori_loop(0, K // 2, products_b, 0)

        share_ma.wait_recv()
        m3b[me_j] = total(m3a, NI)
        share_mb.start()

        @pl.when(s < SWEEPS - 1)
        def _():
            lax.fori_loop(K // 2, K, products_b, 0)

        share_gb.wait_recv()
        unit_b, row_b, col_b = unit(unpack(total(gb, NJ)))
        gram_b[...] = unit_b
        tmp[:R] = jnp.broadcast_to(col_b, (R, 128))
        solve_c = inverse(gram_a * unit_b)
        share_mb.wait_recv()
        c = dot(total(m3b, NJ)[:, :R] * row_b, solve_c, 1, 0, HIGH)
        out_c[...] = c
        set_c(c, row_b)
        for exchange in (scatter1, gather1, scatter2, gather2, share_ga, share_gb, share_ma, share_mb):
            exchange.wait_send()
        return 0

    lax.fori_loop(0, SWEEPS, sweep, 0)
    scale = tmp[:R]
    scale = jnp.concatenate([scale] * 4, axis=1)
    out_b[...] = turned(bt[...] * scale)[:, :R]
    tmp[...] = turned(at[me_j // 2] * scale_a[...])
    out_a[...] = tmp[pl.ds(pl.multiple_of(R * lax.rem(me_j, 2), R), R), :R]


def body(tensor, b_init, c_init):
    vmem = pl.BlockSpec(memory_space=pltpu.VMEM)

    def dma(n):
        return pltpu.SemaphoreType.DMA((n,))

    def slices(n):
        return pltpu.VMEM((n, 32, 128), F32)

    return pl.pallas_call(
        kernel,
        out_shape=(
            jax.ShapeDtypeStruct((R, R), F32),
            jax.ShapeDtypeStruct((COLS, R), F32),
            jax.ShapeDtypeStruct((K, R), F32),
        ),
        in_specs=[pl.BlockSpec(memory_space=pl.ANY), vmem, vmem],
        out_specs=(vmem, vmem, vmem),
        scratch_shapes=[
            pltpu.VMEM((2, ROWS, COLS), F32),
            pltpu.VMEM((K, ROWS, 2 * COLS), BF16),
            pltpu.VMEM((K, ROWS, 128), F32),
            pltpu.VMEM((K, R, COLS), F32),
            pltpu.VMEM((2 * COLS, 128), BF16),
            pltpu.VMEM((2 * R, ROWS), BF16),
            pltpu.VMEM((8, R, 128), F32),
            pltpu.VMEM((R, COLS), F32),
            pltpu.VMEM((K, 128), F32),
            pltpu.VMEM((K, R, 128), F32),
            pltpu.VMEM((R, R), F32),
            pltpu.VMEM((R, R), F32),
            pltpu.VMEM((R, 128), F32),
            pltpu.VMEM((128, 128), F32),
            slices(NJ), slices(NJ), slices(NJ),
            slices(NI), slices(NI), slices(NI),
            slices(NI), slices(NJ),
            pltpu.VMEM((NI, K, 128), F32),
            pltpu.VMEM((NJ, K, 128), F32),
            dma(2),
            dma(NJ), dma(NJ), dma(NJ), dma(NJ),
            dma(NI), dma(NI), dma(NI), dma(NI),
            dma(NI), dma(NI), dma(NJ), dma(NJ),
            dma(NI), dma(NI), dma(NJ), dma(NJ),
        ],
        compiler_params=pltpu.CompilerParams(
            collective_id=0, has_side_effects=True, vmem_limit_bytes=48 * 1024 * 1024
        ),
    )(tensor, b_init, c_init)


def solution(mesh):
    in_specs = (P(None, "ia", "ja"), P("ja", None), P())
    out_specs = (P(("ia", "ja"), None), P("ja", None), P())
    return jax.shard_map(body, mesh=mesh, in_specs=in_specs, out_specs=out_specs, check_vma=False)
```

```python
import functools

import jax
import jax.numpy as jnp
from jax import lax
from jax.experimental import pallas as pl
from jax.experimental.pallas import tpu as pltpu
from jax.sharding import PartitionSpec as P

SWEEPS = 4
K = 8
R = 64
NI = 8
NJ = 16
ROWS = 1024
COLS = 512
HIGH = lax.Precision.HIGHEST
F32 = jnp.float32
BF16 = jnp.bfloat16
MESH = pl.DeviceIdType.MESH


def dot(a, b, ca, cb, precision=None):
    return lax.dot_general(
        a, b, (((ca,), (cb,)), ((), ())), precision=precision, preferred_element_type=F32
    )


def split(x):
    high = x.astype(BF16)
    return high, (x - high.astype(F32)).astype(BF16)


def inverse(a):
    m = 8
    lane = lax.broadcasted_iota(jnp.int32, (m, R), 1)
    sub = lax.broadcasted_iota(jnp.int32, (m, R), 0)
    t = [a[m * i : m * i + m] for i in range(R // m)]

    def rep(v):
        return jnp.broadcast_to(v, (m, R))

    for k0 in range(0, R, m):
        kt = k0 // m
        inside = (lane >= k0) & (lane < k0 + m)
        cols = [[rep(x[:, k0 + j : k0 + j + 1]) for x in t] for j in range(m)]
        panel = jnp.where(inside, jnp.where(lane - k0 == sub, 1.0, 0.0), t[kt])
        block = [cols[j][kt] for j in range(m)]
        for i in range(m):
            p = 1.0 / rep(block[i][i : i + 1, :])
            row = rep(panel[i : i + 1, :]) * p
            f = jnp.where(sub == i, 0.0, block[i])
            panel = jnp.where(sub == i, row, panel) - f * row
            for j in range(i + 1, m):
                row = rep(block[j][i : i + 1, :]) * p
                block[j] = jnp.where(sub == i, row, block[j]) - f * row
        rows = [rep(panel[j : j + 1, :]) for j in range(m)]
        for i in range(R // m):
            if i == kt:
                continue
            even, odd = cols[0][i] * rows[0], cols[1][i] * rows[1]
            for j in range(2, m, 2):
                even, odd = even + cols[j][i] * rows[j], odd + cols[j + 1][i] * rows[j + 1]
            t[i] = jnp.where(inside, 0.0, t[i]) - (even + odd)
        t[kt] = panel
    return jnp.concatenate(t, axis=0)


def pack(gram):
    wide = jnp.concatenate([gram, jnp.zeros((R, 128 - R), F32)], axis=1)
    return wide[:32] + pltpu.roll(wide[32:], 64, 1)


def unpack(x):
    return jnp.concatenate([x[:, :R], pltpu.roll(x, 64, 1)[:, :R]], axis=0)


def diagonal(gram):
    same = lax.broadcasted_iota(jnp.int32, (R, R), 0) == lax.broadcasted_iota(jnp.int32, (R, R), 1)
    only = jnp.where(same, gram, 0.0)
    return jnp.sum(only, axis=0, keepdims=True), jnp.sum(only, axis=1, keepdims=True)


def unit(raw):
    row, col = diagonal(raw)
    row, col = jnp.sqrt(row + 1e-6), jnp.sqrt(col + 1e-6)
    return raw / (col * row), 1.0 / row, 1.0 / col


def turned(x):
    return jnp.concatenate([x, jnp.zeros_like(x)], axis=0).T


class Exchange:
    def __init__(self, axis, n, source, slots, send, recv):
        self.axis, self.n, self.source, self.slots, self.send, self.recv = axis, n, source, slots, send, recv
        self.me = lax.axis_index(axis)

    def copy(self, peer):
        return pltpu.make_async_remote_copy(
            src_ref=self.source(peer),
            dst_ref=self.slots.at[self.me],
            send_sem=self.send.at[peer],
            recv_sem=self.recv.at[self.me],
            device_id={self.axis: peer},
            device_id_type=MESH,
        )

    def start(self, peer):
        self.copy(peer).start()

    def start_all(self):
        for d in range(1, self.n):
            self.start(lax.rem(self.me + d, self.n))

    def wait_from(self, peer):
        pltpu.make_async_remote_copy(
            src_ref=self.source(peer),
            dst_ref=self.slots.at[peer],
            send_sem=self.send.at[peer],
            recv_sem=self.recv.at[peer],
            device_id={self.axis: peer},
            device_id_type=MESH,
        ).wait_recv()

    def wait_all(self):
        for d in range(1, self.n):
            self.wait_from(lax.rem(self.me + d, self.n))

    def wait_sent(self):
        for d in range(1, self.n):
            self.copy(lax.rem(self.me + d, self.n)).wait_send()


def kernel(
    t_hbm, b_hbm, c_hbm, out_a, out_b, out_c,
    b0, c_now, stage, t16, prod, q_ref, m2, w1, at, bt, crow, ccol, gram_b, gram_c, scale_a, scale_b, tmp,
    s1, r1, g1, s2, r2, g2, ga, gb, m3a, m3b,
    load_sem, small_sem, s1s, s1r, g1s, g1r, s2s, s2r, g2s, g2r, gas, gar, gbs, gbr, mas, mar, mbs, mbr,
):
    me_i, me_j = lax.axis_index("ia"), lax.axis_index("ja")
    me_q = me_j // 2
    partner = me_j + 1 - 2 * lax.rem(me_j, 2)

    def load(n):
        k, rows = n // 2, pl.ds(ROWS // 2 * (n % 2), ROWS // 2)
        return pltpu.make_async_copy(t_hbm.at[k, rows], stage.at[k, rows], load_sem.at[n])

    load_b = pltpu.make_async_copy(b_hbm, b0, small_sem.at[0])
    load_c = pltpu.make_async_copy(c_hbm, c_now, small_sem.at[1])
    load_b.start()
    load_c.start()
    for n in range(2 * K):
        load(n).start()

    barrier = pltpu.get_barrier_semaphore()
    for d in range(1, NJ):
        pl.semaphore_signal(barrier, inc=1, device_id={"ja": lax.rem(me_j + d, NJ)}, device_id_type=MESH)
    for d in range(1, NI):
        pl.semaphore_signal(barrier, inc=1, device_id={"ia": lax.rem(me_i + d, NI)}, device_id_type=MESH)

    scatter1 = Exchange("ja", NJ, lambda p: s1.at[p], r1, s1s, s1r)
    gather1 = Exchange("ja", NJ, lambda p: g1.at[me_j], g1, g1s, g1r)
    scatter2 = Exchange("ia", NI, lambda p: s2.at[p], r2, s2s, s2r)
    gather2 = Exchange("ia", NI, lambda p: g2.at[me_i], g2, g2s, g2r)
    share_ga = Exchange("ia", NI, lambda p: ga.at[me_i], ga, gas, gar)
    share_gb = Exchange("ja", NJ, lambda p: gb.at[me_j], gb, gbs, gbr)
    share_ma = Exchange("ia", NI, lambda p: m3a.at[me_i], m3a, mas, mar)
    share_mb = Exchange("ja", NJ, lambda p: m3b.at[me_j], m3b, mbs, mbr)

    def total(ref, n):
        x = ref[0]
        for i in range(1, n):
            x = x + ref[i]
        return x

    def set_w1(b_t):
        high = b_t.astype(BF16).astype(F32)
        both = jnp.concatenate([high, b_t - high], axis=0).T
        w1[:COLS] = both.astype(BF16)
        keep = lax.broadcasted_iota(jnp.int32, (COLS, 128), 1) < R
        w1[COLS:] = jnp.where(keep, both, 0.0).astype(BF16)

    def products_b(k):
        prod[k] = dot(t16[k], w1[...], 1, 0)

    def set_rows(c, inv_norm):
        scaled = c * inv_norm
        crow[...] = jnp.concatenate([scaled, scaled], axis=1)

    def set_c(c):
        wide = jnp.concatenate([c, jnp.zeros((K, 128 - R), F32)], axis=1)
        c_t = jnp.concatenate([wide, jnp.zeros((128 - K, 128), F32)], axis=0).T[:R]
        for k in range(K):
            ccol[k] = jnp.broadcast_to(c_t[:, k : k + 1], (R, 128))
        gram_c[...] = dot(c_t, c_t, 1, 1, HIGH)

    load_b.wait()
    load_c.wait()
    b_t = b0[...]
    set_w1(b_t)
    set_rows(c_now[...], jnp.ones((1, R), F32))
    gb[me_j] = pack(dot(b_t, b_t, 1, 1, HIGH))
    for n in range(2 * K):
        k, rows = n // 2, slice(ROWS // 2 * (n % 2), ROWS // 2 * (n % 2 + 1))
        load(n).wait()
        high, low = split(stage[k, rows])
        t16[k, rows, :COLS] = high
        t16[k, rows, COLS:] = low
        prod[k, rows] = dot(t16[k, rows], w1[...], 1, 0)
        if n == 10:
            pl.semaphore_wait(barrier, NJ - 1 + NI - 1)
            share_gb.start_all()

    def sweep(s, _):
        for e in (4, 5, 3, 6, 2, 7, 1, 0):
            q = lax.rem(me_q + e, 8)
            rows = pl.ds(pl.multiple_of(128 * q, 128), 128)
            acc = prod[0, rows, :] * crow[0:1]
            for k in range(1, K):
                acc = acc + prod[k, rows, :] * crow[k : k + 1]
            acc = acc.T
            acc = acc[:R] + acc[R:]
            s1[2 * q] = acc[:32]
            s1[2 * q + 1] = acc[32:]
            if e:
                scatter1.start(2 * q)
                scatter1.start(2 * q + 1)
            else:
                scatter1.start(partner)
        set_c(c_now[...])
        q_ref[...] = jnp.zeros_like(q_ref)
        m2[...] = jnp.zeros_like(m2)

        @pl.when(s == 0)
        def _():
            share_gb.wait_all()
            gram_b[...] = unpack(total(gb, NJ))
            share_gb.wait_sent()

        @pl.when(s > 0)
        def _():
            share_mb.wait_sent()

        solve_a = inverse(gram_b[...] * gram_c[...])
        scatter1.wait_from(partner)
        acc = s1[me_j] + r1[partner]
        for e in (1, 7, 4, 3, 5, 2, 6):
            for h in range(2):
                j = 2 * lax.rem(me_q + e, 8) + h
                scatter1.wait_from(j)
                acc = acc + r1[j]
        g1[me_j] = acc
        for e in (6, 2, 5, 3, 4, 7, 1):
            for h in range(2):
                gather1.start(2 * lax.rem(me_q + e, 8) + h)
        gather1.start(partner)
        scatter1.wait_sent()

        z, y = me_j // 8, lax.rem(me_j // 4, 2)

        def quarter(n, _):
            g = 2 * lax.rem(z + n // 2, 2) + lax.rem(y + n, 2)
            for e in range(4):

                @pl.when(4 * g + e != me_j)
                def _(e=e):
                    gather1.wait_from(4 * g + e)

            block = jnp.concatenate(
                [
                    jnp.concatenate([g1[4 * g], g1[4 * g + 1]], axis=0),
                    jnp.concatenate([g1[4 * g + 2], g1[4 * g + 3]], axis=0),
                ],
                axis=1,
            )
            block = dot(solve_a, block, 1, 0, HIGH)
            at[g] = block
            both = jnp.concatenate(split(block), axis=0)
            rows = pl.ds(pl.multiple_of(256 * g, 256), 256)
            acc = m2[...]
            for k in range(K):
                x = dot(both, t16[k, rows, :], 1, 0)
                x = x[:R, :COLS] + x[R:, :COLS] + x[:R, COLS:]
                q_ref[k] = q_ref[k] + x
                acc = acc + x * jnp.concatenate([ccol[k]] * 4, axis=1)
            m2[...] = acc
            return 0

        lax.fori_loop(0, 4, quarter, 0)
        for p in range(NI):
            j, h = p // 2, p % 2
            s2[p] = m2[32 * h : 32 * h + 32, 128 * j : 128 * j + 128]
        for d in (6, 2, 5, 3, 7, 1, 4):
            scatter2.start(lax.rem(me_i + d, NI))
        a_t = jnp.concatenate([at[g] for g in range(4)], axis=1)
        ga[me_i] = pack(dot(a_t, a_t, 1, 1, HIGH))
        share_ga.start_all()
        gather1.wait_sent()
        acc = s2[me_i]
        for d in (4, 1, 7, 3, 5, 2, 6):
            j = lax.rem(me_i + d, NI)
            scatter2.wait_from(j)
            acc = acc + r2[j]
        g2[me_i] = acc
        for d in (6, 2, 5, 3, 7, 1, 4):
            gather2.start(lax.rem(me_i + d, NI))
        share_ga.wait_all()
        scatter2.wait_sent()
        gram_a, row_a, col_a = unit(unpack(total(ga, NI)))
        scale_a[...] = jnp.broadcast_to(col_a, (R, 128))
        solve_b = inverse(gram_a * gram_c[...]) * row_a
        gather2.wait_all()
        acc = jnp.concatenate(
            [jnp.concatenate([g2[2 * j], g2[2 * j + 1]], axis=0) for j in range(4)], axis=1
        )
        b_t = dot(solve_b, acc, 1, 0, HIGH)
        bt[...] = b_t

        scaled = b_t * col_a
        lane = lax.broadcasted_iota(jnp.int32, (R, 128), 1)
        sums = jnp.zeros((R, 128), F32)
        for k in range(K):
            x = q_ref[k] * scaled
            x = x[:, :128] + x[:, 128:256] + x[:, 256:384] + x[:, 384:]
            sums = jnp.where(lane == k, jnp.sum(x, axis=1, keepdims=True), sums)
        m3a[me_i] = turned(sums)[:K]
        share_ma.start_all()
        gb[me_j] = pack(dot(b_t, b_t, 1, 1, HIGH))
        share_gb.start_all()

        @pl.when(s < SWEEPS - 1)
        def _():
            set_w1(b_t)
            for k in range(K // 2):
                products_b(k)

        share_ma.wait_all()
        m3b[me_j] = total(m3a, NI)
        share_mb.start_all()

        @pl.when(s < SWEEPS - 1)
        def _():
            for k in range(K // 2, K):
                products_b(k)

        for exchange in (gather2, share_ga, share_ma):
            exchange.wait_sent()
        share_gb.wait_all()
        unit_b, row_b, col_b = unit(unpack(total(gb, NJ)))
        gram_b[...] = unit_b
        scale_b[...] = jnp.broadcast_to(col_b, (R, 128))
        solve_c = inverse(gram_a * unit_b)
        share_gb.wait_sent()
        share_mb.wait_all()
        c = dot(total(m3b, NJ)[:, :R] * row_b, solve_c, 1, 0, HIGH)
        c_now[...] = c
        set_rows(c, row_b)
        return 0

    lax.fori_loop(0, SWEEPS, sweep, 0)
    share_mb.wait_sent()
    out_c[...] = c_now[...]
    out_b[...] = bt[...] * jnp.concatenate([scale_b[...]] * 4, axis=1)
    tmp[...] = turned(at[me_j // 4] * jnp.concatenate([scale_a[...]] * 2, axis=1))
    out_a[...] = tmp[pl.ds(pl.multiple_of(R * lax.rem(me_j, 4), R), R), :R]


def body(tensor, b_init, c_init):
    vmem = pl.BlockSpec(memory_space=pltpu.VMEM)

    def dma(n):
        return pltpu.SemaphoreType.DMA((n,))

    def slices(n):
        return pltpu.VMEM((n, 32, 128), F32)

    a, b, c = pl.pallas_call(
        kernel,
        out_shape=(
            jax.ShapeDtypeStruct((R, R), F32),
            jax.ShapeDtypeStruct((R, COLS), F32),
            jax.ShapeDtypeStruct((K, R), F32),
        ),
        in_specs=[pl.BlockSpec(memory_space=pltpu.HBM)] * 3,
        out_specs=(vmem, vmem, vmem),
        scratch_shapes=[
            pltpu.VMEM((R, COLS), F32),
            pltpu.VMEM((K, R), F32),
            pltpu.VMEM((K, ROWS, COLS), F32),
            pltpu.VMEM((K, ROWS, 2 * COLS), BF16),
            pltpu.VMEM((K, ROWS, 128), F32),
            pltpu.VMEM((K, R, COLS), F32),
            pltpu.VMEM((R, COLS), F32),
            pltpu.VMEM((2 * COLS, 128), BF16),
            pltpu.VMEM((4, R, 256), F32),
            pltpu.VMEM((R, COLS), F32),
            pltpu.VMEM((K, 128), F32),
            pltpu.VMEM((K, R, 128), F32),
            pltpu.VMEM((R, R), F32),
            pltpu.VMEM((R, R), F32),
            pltpu.VMEM((R, 128), F32),
            pltpu.VMEM((R, 128), F32),
            pltpu.VMEM((256, 128), F32),
            slices(NJ), slices(NJ), slices(NJ),
            slices(NI), slices(NI), slices(NI),
            slices(NI), slices(NJ),
            pltpu.VMEM((NI, K, 128), F32),
            pltpu.VMEM((NJ, K, 128), F32),
            dma(2 * K), dma(2),
            dma(NJ), dma(NJ), dma(NJ), dma(NJ),
            dma(NI), dma(NI), dma(NI), dma(NI),
            dma(NI), dma(NI), dma(NJ), dma(NJ),
            dma(NI), dma(NI), dma(NJ), dma(NJ),
        ],
        compiler_params=pltpu.CompilerParams(
            collective_id=0, has_side_effects=True, vmem_limit_bytes=48 * 1024 * 1024
        ),
    )(tensor, b_init.T, c_init)
    return a, b.T, c


def solution(mesh):
    in_specs = (P(None, "ia", "ja"), P("ja", None), P())
    out_specs = (P(("ia", "ja"), None), P("ja", None), P())
    return jax.shard_map(body, mesh=mesh, in_specs=in_specs, out_specs=out_specs, check_vma=False)
```

```python
import functools

import jax
import jax.numpy as jnp
from jax import lax
from jax.experimental import pallas as pl
from jax.experimental.pallas import tpu as pltpu
from jax.sharding import PartitionSpec as P

SWEEPS = 4
K = 8
R = 64
NI = 8
NJ = 16
ROWS = 1024
COLS = 512
HIGH = lax.Precision.HIGHEST
F32 = jnp.float32
BF16 = jnp.bfloat16
MESH = pl.DeviceIdType.MESH


def dot(a, b, ca, cb, precision=None):
    return lax.dot_general(
        a, b, (((ca,), (cb,)), ((), ())), precision=precision, preferred_element_type=F32
    )


def split(x):
    high = x.astype(BF16)
    return high, (x - high.astype(F32)).astype(BF16)


def inverse(a):
    m = 8
    lane = lax.broadcasted_iota(jnp.int32, (m, R), 1)
    sub = lax.broadcasted_iota(jnp.int32, (m, R), 0)
    t = [a[m * i : m * i + m] for i in range(R // m)]

    def rep(v):
        return jnp.broadcast_to(v, (m, R))

    for k0 in range(0, R, m):
        kt = k0 // m
        inside = (lane >= k0) & (lane < k0 + m)
        cols = [[rep(x[:, k0 + j : k0 + j + 1]) for x in t] for j in range(m)]
        panel = jnp.where(inside, jnp.where(lane - k0 == sub, 1.0, 0.0), t[kt])
        block = [cols[j][kt] for j in range(m)]
        for i in range(m):
            p = 1.0 / rep(block[i][i : i + 1, :])
            row = rep(panel[i : i + 1, :]) * p
            f = jnp.where(sub == i, 0.0, block[i])
            panel = jnp.where(sub == i, row, panel) - f * row
            for j in range(i + 1, m):
                row = rep(block[j][i : i + 1, :]) * p
                block[j] = jnp.where(sub == i, row, block[j]) - f * row
        rows = [rep(panel[j : j + 1, :]) for j in range(m)]
        for i in range(R // m):
            if i == kt:
                continue
            even, odd = cols[0][i] * rows[0], cols[1][i] * rows[1]
            for j in range(2, m, 2):
                even, odd = even + cols[j][i] * rows[j], odd + cols[j + 1][i] * rows[j + 1]
            t[i] = jnp.where(inside, 0.0, t[i]) - (even + odd)
        t[kt] = panel
    return jnp.concatenate(t, axis=0)


def pack(gram):
    wide = jnp.concatenate([gram, jnp.zeros((R, 128 - R), F32)], axis=1)
    return wide[:32] + pltpu.roll(wide[32:], 64, 1)


def unpack(x):
    return jnp.concatenate([x[:, :R], pltpu.roll(x, 64, 1)[:, :R]], axis=0)


def diagonal(gram):
    same = lax.broadcasted_iota(jnp.int32, (R, R), 0) == lax.broadcasted_iota(jnp.int32, (R, R), 1)
    only = jnp.where(same, gram, 0.0)
    return jnp.sum(only, axis=0, keepdims=True), jnp.sum(only, axis=1, keepdims=True)


def unit(raw):
    row, col = diagonal(raw)
    row, col = jnp.sqrt(row + 1e-6), jnp.sqrt(col + 1e-6)
    return raw / (col * row), 1.0 / row, 1.0 / col


def turned(x):
    return jnp.concatenate([x, jnp.zeros_like(x)], axis=0).T


class Exchange:
    def __init__(self, axis, n, source, slots, send, recv):
        self.axis, self.n, self.source, self.slots, self.send, self.recv = axis, n, source, slots, send, recv
        self.me = lax.axis_index(axis)

    def copy(self, peer):
        return pltpu.make_async_remote_copy(
            src_ref=self.source(peer),
            dst_ref=self.slots.at[self.me],
            send_sem=self.send.at[peer],
            recv_sem=self.recv.at[self.me],
            device_id={self.axis: peer},
            device_id_type=MESH,
        )

    def start(self, peer):
        self.copy(peer).start()

    def start_all(self):
        for d in range(1, self.n):
            self.start(lax.rem(self.me + d, self.n))

    def wait_from(self, peer):
        pltpu.make_async_remote_copy(
            src_ref=self.source(peer),
            dst_ref=self.slots.at[peer],
            send_sem=self.send.at[peer],
            recv_sem=self.recv.at[peer],
            device_id={self.axis: peer},
            device_id_type=MESH,
        ).wait_recv()

    def wait_all(self):
        for d in range(1, self.n):
            self.wait_from(lax.rem(self.me + d, self.n))

    def wait_sent(self):
        for d in range(1, self.n):
            self.copy(lax.rem(self.me + d, self.n)).wait_send()


def kernel(
    t_hbm, b_hbm, c_hbm, out_a, out_b, out_c,
    b0, c_now, stage, t16, prod, q_ref, m2, w1, at, bt, crow, ccol, gram_b, gram_c, scale_a, scale_b, tmp,
    s1, r1, g1, s2, r2, g2, ga, gb, m3a, m3b,
    load_sem, small_sem, s1s, s1r, g1s, g1r, s2s, s2r, g2s, g2r, gas, gar, gbs, gbr, mas, mar, mbs, mbr,
):
    me_i, me_j = lax.axis_index("ia"), lax.axis_index("ja")
    me_q = me_j // 2
    partner = me_j + 1 - 2 * lax.rem(me_j, 2)

    def load(n):
        k, rows = n // 2, pl.ds(ROWS // 2 * (n % 2), ROWS // 2)
        return pltpu.make_async_copy(t_hbm.at[k, rows], stage.at[k, rows], load_sem.at[n])

    load_b = pltpu.make_async_copy(b_hbm, b0, small_sem.at[0])
    load_c = pltpu.make_async_copy(c_hbm, c_now, small_sem.at[1])
    load_b.start()
    load_c.start()
    for n in range(2 * K):
        load(n).start()

    barrier = pltpu.get_barrier_semaphore()
    for d in range(1, NJ):
        pl.semaphore_signal(barrier, inc=1, device_id={"ja": lax.rem(me_j + d, NJ)}, device_id_type=MESH)
    for d in range(1, NI):
        pl.semaphore_signal(barrier, inc=1, device_id={"ia": lax.rem(me_i + d, NI)}, device_id_type=MESH)

    scatter1 = Exchange("ja", NJ, lambda p: s1.at[p], r1, s1s, s1r)
    gather1 = Exchange("ja", NJ, lambda p: g1.at[me_j], g1, g1s, g1r)
    scatter2 = Exchange("ia", NI, lambda p: s2.at[p], r2, s2s, s2r)
    gather2 = Exchange("ia", NI, lambda p: g2.at[me_i], g2, g2s, g2r)
    share_ga = Exchange("ia", NI, lambda p: ga.at[me_i], ga, gas, gar)
    share_gb = Exchange("ja", NJ, lambda p: gb.at[me_j], gb, gbs, gbr)
    share_ma = Exchange("ia", NI, lambda p: m3a.at[me_i], m3a, mas, mar)
    share_mb = Exchange("ja", NJ, lambda p: m3b.at[me_j], m3b, mbs, mbr)

    def total(ref, n):
        x = ref[0]
        for i in range(1, n):
            x = x + ref[i]
        return x

    def set_w1(b_t):
        high = b_t.astype(BF16).astype(F32)
        both = jnp.concatenate([high, b_t - high], axis=0).T
        w1[:COLS] = both.astype(BF16)
        keep = lax.broadcasted_iota(jnp.int32, (COLS, 128), 1) < R
        w1[COLS:] = jnp.where(keep, both, 0.0).astype(BF16)

    def products_b(k):
        prod[k] = dot(t16[k], w1[...], 1, 0)

    def set_rows(c, inv_norm):
        scaled = c * inv_norm
        crow[...] = jnp.concatenate([scaled, scaled], axis=1)

    def set_c(c):
        wide = jnp.concatenate([c, jnp.zeros((K, 128 - R), F32)], axis=1)
        c_t = jnp.concatenate([wide, jnp.zeros((128 - K, 128), F32)], axis=0).T[:R]
        for k in range(K):
            ccol[k] = jnp.broadcast_to(c_t[:, k : k + 1], (R, 128))
        gram_c[...] = dot(c_t, c_t, 1, 1, HIGH)

    load_b.wait()
    load_c.wait()
    b_t = b0[...]
    set_w1(b_t)
    set_rows(c_now[...], jnp.ones((1, R), F32))
    gb[me_j] = pack(dot(b_t, b_t, 1, 1, HIGH))
    for n in range(2 * K):
        k, rows = n // 2, slice(ROWS // 2 * (n % 2), ROWS // 2 * (n % 2 + 1))
        load(n).wait()
        for half in range(2):
            part = slice(rows.start + ROWS // 4 * half, rows.start + ROWS // 4 * (half + 1))
            high, low = split(stage[k, part])
            t16[k, part, :COLS] = high
            t16[k, part, COLS:] = low
            prod[k, part] = dot(high, w1[:COLS], 1, 0) + dot(low, w1[COLS:], 1, 0)
        if n == 8:
            pl.semaphore_wait(barrier, NJ - 1 + NI - 1)
            share_gb.start_all()

    def sweep(s, _):
        for e in (4, 5, 3, 6, 2, 7, 1, 0):
            q = lax.rem(me_q + e, 8)
            rows = pl.ds(pl.multiple_of(128 * q, 128), 128)
            acc = prod[0, rows, :] * crow[0:1]
            for k in range(1, K):
                acc = acc + prod[k, rows, :] * crow[k : k + 1]
            acc = acc.T
            acc = acc[:R] + acc[R:]
            s1[2 * q] = acc[:32]
            s1[2 * q + 1] = acc[32:]
            if e:
                scatter1.start(2 * q)
                scatter1.start(2 * q + 1)
            else:
                scatter1.start(partner)
        set_c(c_now[...])
        q_ref[...] = jnp.zeros_like(q_ref)
        m2[...] = jnp.zeros_like(m2)

        @pl.when(s == 0)
        def _():
            share_gb.wait_all()
            gram_b[...] = unpack(total(gb, NJ))
            share_gb.wait_sent()

        @pl.when(s > 0)
        def _():
            share_mb.wait_sent()

        solve_a = inverse(gram_b[...] * gram_c[...])
        scatter1.wait_from(partner)
        acc = s1[me_j] + r1[partner]
        for e in (1, 7, 4, 3, 5, 2, 6):
            for h in range(2):
                j = 2 * lax.rem(me_q + e, 8) + h
                scatter1.wait_from(j)
                acc = acc + r1[j]
        g1[me_j] = acc
        for e in (6, 2, 5, 3, 4, 7, 1):
            for h in range(2):
                gather1.start(2 * lax.rem(me_q + e, 8) + h)
        gather1.start(partner)
        scatter1.wait_sent()

        z, y = me_j // 8, lax.rem(me_j // 4, 2)

        def quarter(n, _):
            g = 2 * lax.rem(z + n // 2, 2) + lax.rem(y + n, 2)
            for e in range(4):

                @pl.when(4 * g + e != me_j)
                def _(e=e):
                    gather1.wait_from(4 * g + e)

            block = jnp.concatenate(
                [
                    jnp.concatenate([g1[4 * g], g1[4 * g + 1]], axis=0),
                    jnp.concatenate([g1[4 * g + 2], g1[4 * g + 3]], axis=0),
                ],
                axis=1,
            )
            block = dot(solve_a, block, 1, 0, HIGH)
            at[g] = block
            both = jnp.concatenate(split(block), axis=0)
            rows = pl.ds(pl.multiple_of(256 * g, 256), 256)
            acc = m2[...]
            for k in range(K):
                x = dot(both, t16[k, rows, :], 1, 0)
                x = x[:R, :COLS] + x[R:, :COLS] + x[:R, COLS:]
                q_ref[k] = q_ref[k] + x
                acc = acc + x * jnp.concatenate([ccol[k]] * 4, axis=1)
            m2[...] = acc
            return 0

        lax.fori_loop(0, 4, quarter, 0)
        for p in range(NI):
            j, h = p // 2, p % 2
            s2[p] = m2[32 * h : 32 * h + 32, 128 * j : 128 * j + 128]
        for d in (6, 2, 5, 3, 7, 1, 4):
            scatter2.start(lax.rem(me_i + d, NI))
        a_t = jnp.concatenate([at[g] for g in range(4)], axis=1)
        ga[me_i] = pack(dot(a_t, a_t, 1, 1, HIGH))
        share_ga.start_all()
        gather1.wait_sent()
        acc = s2[me_i]
        for d in (4, 1, 7, 3, 5, 2, 6):
            j = lax.rem(me_i + d, NI)
            scatter2.wait_from(j)
            acc = acc + r2[j]
        g2[me_i] = acc
        for d in (6, 2, 5, 3, 7, 1, 4):
            gather2.start(lax.rem(me_i + d, NI))
        share_ga.wait_all()
        scatter2.wait_sent()
        gram_a, row_a, col_a = unit(unpack(total(ga, NI)))
        scale_a[...] = jnp.broadcast_to(col_a, (R, 128))
        solve_b = inverse(gram_a * gram_c[...]) * row_a
        gather2.wait_all()
        acc = jnp.concatenate(
            [jnp.concatenate([g2[2 * j], g2[2 * j + 1]], axis=0) for j in range(4)], axis=1
        )
        b_t = dot(solve_b, acc, 1, 0, HIGH)
        bt[...] = b_t

        scaled = b_t * col_a
        lane = lax.broadcasted_iota(jnp.int32, (R, 128), 1)
        sums = jnp.zeros((R, 128), F32)
        for k in range(K):
            x = q_ref[k] * scaled
            x = x[:, :128] + x[:, 128:256] + x[:, 256:384] + x[:, 384:]
            sums = jnp.where(lane == k, jnp.sum(x, axis=1, keepdims=True), sums)
        m3a[me_i] = turned(sums)[:K]
        share_ma.start_all()
        gb[me_j] = pack(dot(b_t, b_t, 1, 1, HIGH))
        share_gb.start_all()

        @pl.when(s < SWEEPS - 1)
        def _():
            set_w1(b_t)
            for k in range(K // 2):
                products_b(k)

        share_ma.wait_all()
        m3b[me_j] = total(m3a, NI)
        share_mb.start_all()

        @pl.when(s < SWEEPS - 1)
        def _():
            for k in range(K // 2, K):
                products_b(k)

        for exchange in (gather2, share_ga, share_ma):
            exchange.wait_sent()
        share_gb.wait_all()
        unit_b, row_b, col_b = unit(unpack(total(gb, NJ)))
        gram_b[...] = unit_b
        scale_b[...] = jnp.broadcast_to(col_b, (R, 128))
        solve_c = inverse(gram_a * unit_b)
        share_gb.wait_sent()
        share_mb.wait_all()
        c = dot(total(m3b, NJ)[:, :R] * row_b, solve_c, 1, 0, HIGH)
        c_now[...] = c
        set_rows(c, row_b)
        return 0

    lax.fori_loop(0, SWEEPS, sweep, 0)
    share_mb.wait_sent()
    out_c[...] = c_now[...]
    out_b[...] = bt[...] * jnp.concatenate([scale_b[...]] * 4, axis=1)
    tmp[...] = turned(at[me_j // 4] * jnp.concatenate([scale_a[...]] * 2, axis=1))
    out_a[...] = tmp[pl.ds(pl.multiple_of(R * lax.rem(me_j, 4), R), R), :R]


def body(tensor, b_init, c_init):
    vmem = pl.BlockSpec(memory_space=pltpu.VMEM)

    def dma(n):
        return pltpu.SemaphoreType.DMA((n,))

    def slices(n):
        return pltpu.VMEM((n, 32, 128), F32)

    a, b, c = pl.pallas_call(
        kernel,
        out_shape=(
            jax.ShapeDtypeStruct((R, R), F32),
            jax.ShapeDtypeStruct((R, COLS), F32),
            jax.ShapeDtypeStruct((K, R), F32),
        ),
        in_specs=[pl.BlockSpec(memory_space=pltpu.HBM)] * 3,
        out_specs=(vmem, vmem, vmem),
        scratch_shapes=[
            pltpu.VMEM((R, COLS), F32),
            pltpu.VMEM((K, R), F32),
            pltpu.VMEM((K, ROWS, COLS), F32),
            pltpu.VMEM((K, ROWS, 2 * COLS), BF16),
            pltpu.VMEM((K, ROWS, 128), F32),
            pltpu.VMEM((K, R, COLS), F32),
            pltpu.VMEM((R, COLS), F32),
            pltpu.VMEM((2 * COLS, 128), BF16),
            pltpu.VMEM((4, R, 256), F32),
            pltpu.VMEM((R, COLS), F32),
            pltpu.VMEM((K, 128), F32),
            pltpu.VMEM((K, R, 128), F32),
            pltpu.VMEM((R, R), F32),
            pltpu.VMEM((R, R), F32),
            pltpu.VMEM((R, 128), F32),
            pltpu.VMEM((R, 128), F32),
            pltpu.VMEM((256, 128), F32),
            slices(NJ), slices(NJ), slices(NJ),
            slices(NI), slices(NI), slices(NI),
            slices(NI), slices(NJ),
            pltpu.VMEM((NI, K, 128), F32),
            pltpu.VMEM((NJ, K, 128), F32),
            dma(2 * K), dma(2),
            dma(NJ), dma(NJ), dma(NJ), dma(NJ),
            dma(NI), dma(NI), dma(NI), dma(NI),
            dma(NI), dma(NI), dma(NJ), dma(NJ),
            dma(NI), dma(NI), dma(NJ), dma(NJ),
        ],
        compiler_params=pltpu.CompilerParams(
            collective_id=0, has_side_effects=True, vmem_limit_bytes=48 * 1024 * 1024
        ),
    )(tensor, b_init.T, c_init)
    return a, b.T, c


def solution(mesh):
    in_specs = (P(None, "ia", "ja"), P("ja", None), P())
    out_specs = (P(("ia", "ja"), None), P("ja", None), P())
    return jax.shard_map(body, mesh=mesh, in_specs=in_specs, out_specs=out_specs, check_vma=False)
```

```python
import functools

import jax
import jax.numpy as jnp
from jax import lax
from jax.experimental import pallas as pl
from jax.experimental.pallas import tpu as pltpu
from jax.sharding import PartitionSpec as P

SWEEPS = 4
K = 8
R = 64
NI = 8
NJ = 16
ROWS = 1024
COLS = 512
HIGH = lax.Precision.HIGHEST
F32 = jnp.float32
BF16 = jnp.bfloat16
MESH = pl.DeviceIdType.MESH


def dot(a, b, ca, cb, precision=None):
    return lax.dot_general(
        a, b, (((ca,), (cb,)), ((), ())), precision=precision, preferred_element_type=F32
    )


def split(x):
    high = x.astype(BF16)
    return high, (x - high.astype(F32)).astype(BF16)


def inverse(a):
    m = 8
    lane = lax.broadcasted_iota(jnp.int32, (m, R), 1)
    sub = lax.broadcasted_iota(jnp.int32, (m, R), 0)
    t = [a[m * i : m * i + m] for i in range(R // m)]

    def rep(v):
        return jnp.broadcast_to(v, (m, R))

    for k0 in range(0, R, m):
        kt = k0 // m
        inside = (lane >= k0) & (lane < k0 + m)
        cols = [[rep(x[:, k0 + j : k0 + j + 1]) for x in t] for j in range(m)]
        panel = jnp.where(inside, jnp.where(lane - k0 == sub, 1.0, 0.0), t[kt])
        block = [cols[j][kt] for j in range(m)]
        for i in range(m):
            p = 1.0 / rep(block[i][i : i + 1, :])
            row = rep(panel[i : i + 1, :]) * p
            f = jnp.where(sub == i, 0.0, block[i])
            panel = jnp.where(sub == i, row, panel) - f * row
            for j in range(i + 1, m):
                row = rep(block[j][i : i + 1, :]) * p
                block[j] = jnp.where(sub == i, row, block[j]) - f * row
        rows = [rep(panel[j : j + 1, :]) for j in range(m)]
        for i in range(R // m):
            if i == kt:
                continue
            even, odd = cols[0][i] * rows[0], cols[1][i] * rows[1]
            for j in range(2, m, 2):
                even, odd = even + cols[j][i] * rows[j], odd + cols[j + 1][i] * rows[j + 1]
            t[i] = jnp.where(inside, 0.0, t[i]) - (even + odd)
        t[kt] = panel
    return jnp.concatenate(t, axis=0)


def pack(gram):
    wide = jnp.concatenate([gram, jnp.zeros((R, 128 - R), F32)], axis=1)
    return wide[:32] + pltpu.roll(wide[32:], 64, 1)


def unpack(x):
    return jnp.concatenate([x[:, :R], pltpu.roll(x, 64, 1)[:, :R]], axis=0)


def diagonal(gram):
    same = lax.broadcasted_iota(jnp.int32, (R, R), 0) == lax.broadcasted_iota(jnp.int32, (R, R), 1)
    only = jnp.where(same, gram, 0.0)
    return jnp.sum(only, axis=0, keepdims=True), jnp.sum(only, axis=1, keepdims=True)


def unit(raw):
    row, col = diagonal(raw)
    row, col = jnp.sqrt(row + 1e-6), jnp.sqrt(col + 1e-6)
    return raw / (col * row), 1.0 / row, 1.0 / col


def turned(x):
    return jnp.concatenate([x, jnp.zeros_like(x)], axis=0).T


class Exchange:
    def __init__(self, axis, n, source, slots, send, recv):
        self.axis, self.n, self.source, self.slots, self.send, self.recv = axis, n, source, slots, send, recv
        self.me = lax.axis_index(axis)

    def copy(self, peer):
        return pltpu.make_async_remote_copy(
            src_ref=self.source(peer),
            dst_ref=self.slots.at[self.me],
            send_sem=self.send.at[peer],
            recv_sem=self.recv.at[self.me],
            device_id={self.axis: peer},
            device_id_type=MESH,
        )

    def start(self, peer):
        self.copy(peer).start()

    def start_all(self):
        for d in range(1, self.n):
            self.start(lax.rem(self.me + d, self.n))

    def wait_from(self, peer):
        pltpu.make_async_remote_copy(
            src_ref=self.source(peer),
            dst_ref=self.slots.at[peer],
            send_sem=self.send.at[peer],
            recv_sem=self.recv.at[peer],
            device_id={self.axis: peer},
            device_id_type=MESH,
        ).wait_recv()

    def wait_all(self):
        for d in range(1, self.n):
            self.wait_from(lax.rem(self.me + d, self.n))

    def wait_sent(self):
        for d in range(1, self.n):
            self.copy(lax.rem(self.me + d, self.n)).wait_send()


def kernel(
    t_hbm, b_hbm, c_hbm, out_a, out_b, out_c,
    b0, c_now, stage, t16, prod, q_ref, m2, w1, at, bt, crow, ccol, gram_b, gram_c, scale_a, scale_b, tmp,
    s1, r1, g1, s2, r2, g2, ga, gb, m3a, m3b,
    load_sem, small_sem, s1s, s1r, g1s, g1r, s2s, s2r, g2s, g2r, gas, gar, gbs, gbr, mas, mar, mbs, mbr,
):
    me_i, me_j = lax.axis_index("ia"), lax.axis_index("ja")
    me_q = me_j // 2
    partner = me_j + 1 - 2 * lax.rem(me_j, 2)

    def load(n):
        k, rows = n // 2, pl.ds(ROWS // 2 * (n % 2), ROWS // 2)
        return pltpu.make_async_copy(t_hbm.at[k, rows], stage.at[k, rows], load_sem.at[n])

    load_b = pltpu.make_async_copy(b_hbm, b0, small_sem.at[0])
    load_c = pltpu.make_async_copy(c_hbm, c_now, small_sem.at[1])
    load_b.start()
    load_c.start()
    for n in range(2 * K):
        load(n).start()

    barrier = pltpu.get_barrier_semaphore()
    for d in range(1, NJ):
        pl.semaphore_signal(barrier, inc=1, device_id={"ja": lax.rem(me_j + d, NJ)}, device_id_type=MESH)
    for d in range(1, NI):
        pl.semaphore_signal(barrier, inc=1, device_id={"ia": lax.rem(me_i + d, NI)}, device_id_type=MESH)

    scatter1 = Exchange("ja", NJ, lambda p: s1.at[p], r1, s1s, s1r)
    gather1 = Exchange("ja", NJ, lambda p: g1.at[me_j], g1, g1s, g1r)
    scatter2 = Exchange("ia", NI, lambda p: s2.at[p], r2, s2s, s2r)
    gather2 = Exchange("ia", NI, lambda p: g2.at[me_i], g2, g2s, g2r)
    share_ga = Exchange("ia", NI, lambda p: ga.at[me_i], ga, gas, gar)
    share_gb = Exchange("ja", NJ, lambda p: gb.at[me_j], gb, gbs, gbr)
    share_ma = Exchange("ia", NI, lambda p: m3a.at[me_i], m3a, mas, mar)
    share_mb = Exchange("ja", NJ, lambda p: m3b.at[me_j], m3b, mbs, mbr)

    def total(ref, n):
        x = ref[0]
        for i in range(1, n):
            x = x + ref[i]
        return x

    def set_w1(b_t):
        high = b_t.astype(BF16).astype(F32)
        both = jnp.concatenate([high, b_t - high], axis=0).T
        w1[:COLS] = both.astype(BF16)
        keep = lax.broadcasted_iota(jnp.int32, (COLS, 128), 1) < R
        w1[COLS:] = jnp.where(keep, both, 0.0).astype(BF16)

    def products_b(k):
        prod[k] = dot(t16[k], w1[...], 1, 0)

    def set_rows(c, inv_norm):
        scaled = c * inv_norm
        crow[...] = jnp.concatenate([scaled, scaled], axis=1)

    def set_c(c):
        wide = jnp.concatenate([c, jnp.zeros((K, 128 - R), F32)], axis=1)
        c_t = jnp.concatenate([wide, jnp.zeros((128 - K, 128), F32)], axis=0).T[:R]
        for k in range(K):
            ccol[k] = jnp.broadcast_to(c_t[:, k : k + 1], (R, 128))
        gram_c[...] = dot(c_t, c_t, 1, 1, HIGH)

    load_b.wait()
    load_c.wait()
    b_t = b0[...]
    set_w1(b_t)
    set_rows(c_now[...], jnp.ones((1, R), F32))
    gb[me_j] = pack(dot(b_t, b_t, 1, 1, HIGH))
    for n in range(2 * K):
        k, rows = n // 2, slice(ROWS // 2 * (n % 2), ROWS // 2 * (n % 2 + 1))
        load(n).wait()
        for piece in range(4):
            part = slice(rows.start + ROWS // 8 * piece, rows.start + ROWS // 8 * (piece + 1))
            high, low = split(stage[k, part])
            t16[k, part, :COLS] = high
            t16[k, part, COLS:] = low
            prod[k, part] = dot(high, w1[:COLS], 1, 0) + dot(low, w1[COLS:], 1, 0)
        if n == 8:
            pl.semaphore_wait(barrier, NJ - 1 + NI - 1)
            share_gb.start_all()

    def sweep(s, _):
        for e in (4, 5, 3, 6, 2, 7, 1, 0):
            q = lax.rem(me_q + e, 8)
            rows = pl.ds(pl.multiple_of(128 * q, 128), 128)
            acc = prod[0, rows, :] * crow[0:1]
            for k in range(1, K):
                acc = acc + prod[k, rows, :] * crow[k : k + 1]
            acc = acc.T
            acc = acc[:R] + acc[R:]
            s1[2 * q] = acc[:32]
            s1[2 * q + 1] = acc[32:]
            if e:
                scatter1.start(2 * q)
                scatter1.start(2 * q + 1)
            else:
                scatter1.start(partner)
        set_c(c_now[...])
        q_ref[...] = jnp.zeros_like(q_ref)
        m2[...] = jnp.zeros_like(m2)

        @pl.when(s == 0)
        def _():
            share_gb.wait_all()
            gram_b[...] = unpack(total(gb, NJ))
            share_gb.wait_sent()

        @pl.when(s > 0)
        def _():
            share_mb.wait_sent()

        solve_a = inverse(gram_b[...] * gram_c[...])
        scatter1.wait_from(partner)
        acc = s1[me_j] + r1[partner]
        for e in (1, 7, 4, 3, 5, 2, 6):
            for h in range(2):
                j = 2 * lax.rem(me_q + e, 8) + h
                scatter1.wait_from(j)
                acc = acc + r1[j]
        g1[me_j] = acc
        for e in (6, 2, 5, 3, 4, 7, 1):
            for h in range(2):
                gather1.start(2 * lax.rem(me_q + e, 8) + h)
        gather1.start(partner)
        scatter1.wait_sent()

        z, y = me_j // 8, lax.rem(me_j // 4, 2)

        def quarter(n, _):
            g = 2 * lax.rem(z + n // 2, 2) + lax.rem(y + n, 2)
            for e in range(4):

                @pl.when(4 * g + e != me_j)
                def _(e=e):
                    gather1.wait_from(4 * g + e)

            block = jnp.concatenate(
                [
                    jnp.concatenate([g1[4 * g], g1[4 * g + 1]], axis=0),
                    jnp.concatenate([g1[4 * g + 2], g1[4 * g + 3]], axis=0),
                ],
                axis=1,
            )
            block = dot(solve_a, block, 1, 0, HIGH)
            at[g] = block
            both = jnp.concatenate(split(block), axis=0)
            rows = pl.ds(pl.multiple_of(256 * g, 256), 256)
            acc = m2[...]
            for k in range(K):
                x = dot(both, t16[k, rows, :], 1, 0)
                x = x[:R, :COLS] + x[R:, :COLS] + x[:R, COLS:]
                q_ref[k] = q_ref[k] + x
                acc = acc + x * jnp.concatenate([ccol[k]] * 4, axis=1)
            m2[...] = acc
            return 0

        lax.fori_loop(0, 4, quarter, 0)
        for p in range(NI):
            j, h = p // 2, p % 2
            s2[p] = m2[32 * h : 32 * h + 32, 128 * j : 128 * j + 128]
        for d in (6, 2, 5, 3, 7, 1, 4):
            scatter2.start(lax.rem(me_i + d, NI))
        a_t = jnp.concatenate([at[g] for g in range(4)], axis=1)
        ga[me_i] = pack(dot(a_t, a_t, 1, 1, HIGH))
        share_ga.start_all()
        gather1.wait_sent()
        acc = s2[me_i]
        for d in (4, 1, 7, 3, 5, 2, 6):
            j = lax.rem(me_i + d, NI)
            scatter2.wait_from(j)
            acc = acc + r2[j]
        g2[me_i] = acc
        for d in (6, 2, 5, 3, 7, 1, 4):
            gather2.start(lax.rem(me_i + d, NI))
        share_ga.wait_all()
        scatter2.wait_sent()
        gram_a, row_a, col_a = unit(unpack(total(ga, NI)))
        scale_a[...] = jnp.broadcast_to(col_a, (R, 128))
        solve_b = inverse(gram_a * gram_c[...]) * row_a
        gather2.wait_all()
        acc = jnp.concatenate(
            [jnp.concatenate([g2[2 * j], g2[2 * j + 1]], axis=0) for j in range(4)], axis=1
        )
        b_t = dot(solve_b, acc, 1, 0, HIGH)
        bt[...] = b_t

        scaled = b_t * col_a
        lane = lax.broadcasted_iota(jnp.int32, (R, 128), 1)
        sums = jnp.zeros((R, 128), F32)
        for k in range(K):
            x = q_ref[k] * scaled
            x = x[:, :128] + x[:, 128:256] + x[:, 256:384] + x[:, 384:]
            sums = jnp.where(lane == k, jnp.sum(x, axis=1, keepdims=True), sums)
        m3a[me_i] = turned(sums)[:K]
        share_ma.start_all()
        gb[me_j] = pack(dot(b_t, b_t, 1, 1, HIGH))
        share_gb.start_all()

        @pl.when(s < SWEEPS - 1)
        def _():
            set_w1(b_t)
            for k in range(K // 2):
                products_b(k)

        share_ma.wait_all()
        m3b[me_j] = total(m3a, NI)
        share_mb.start_all()

        @pl.when(s < SWEEPS - 1)
        def _():
            for k in range(K // 2, K):
                products_b(k)

        for exchange in (gather2, share_ga, share_ma):
            exchange.wait_sent()
        share_gb.wait_all()
        unit_b, row_b, col_b = unit(unpack(total(gb, NJ)))
        gram_b[...] = unit_b
        scale_b[...] = jnp.broadcast_to(col_b, (R, 128))
        solve_c = inverse(gram_a * unit_b)
        share_gb.wait_sent()
        share_mb.wait_all()
        c = dot(total(m3b, NJ)[:, :R] * row_b, solve_c, 1, 0, HIGH)
        c_now[...] = c
        set_rows(c, row_b)
        return 0

    lax.fori_loop(0, SWEEPS, sweep, 0)
    share_mb.wait_sent()
    out_c[...] = c_now[...]
    out_b[...] = bt[...] * jnp.concatenate([scale_b[...]] * 4, axis=1)
    tmp[...] = turned(at[me_j // 4] * jnp.concatenate([scale_a[...]] * 2, axis=1))
    out_a[...] = tmp[pl.ds(pl.multiple_of(R * lax.rem(me_j, 4), R), R), :R]


def body(tensor, b_init, c_init):
    vmem = pl.BlockSpec(memory_space=pltpu.VMEM)

    def dma(n):
        return pltpu.SemaphoreType.DMA((n,))

    def slices(n):
        return pltpu.VMEM((n, 32, 128), F32)

    a, b, c = pl.pallas_call(
        kernel,
        out_shape=(
            jax.ShapeDtypeStruct((R, R), F32),
            jax.ShapeDtypeStruct((R, COLS), F32),
            jax.ShapeDtypeStruct((K, R), F32),
        ),
        in_specs=[pl.BlockSpec(memory_space=pltpu.HBM)] * 3,
        out_specs=(vmem, vmem, vmem),
        scratch_shapes=[
            pltpu.VMEM((R, COLS), F32),
            pltpu.VMEM((K, R), F32),
            pltpu.VMEM((K, ROWS, COLS), F32),
            pltpu.VMEM((K, ROWS, 2 * COLS), BF16),
            pltpu.VMEM((K, ROWS, 128), F32),
            pltpu.VMEM((K, R, COLS), F32),
            pltpu.VMEM((R, COLS), F32),
            pltpu.VMEM((2 * COLS, 128), BF16),
            pltpu.VMEM((4, R, 256), F32),
            pltpu.VMEM((R, COLS), F32),
            pltpu.VMEM((K, 128), F32),
            pltpu.VMEM((K, R, 128), F32),
            pltpu.VMEM((R, R), F32),
            pltpu.VMEM((R, R), F32),
            pltpu.VMEM((R, 128), F32),
            pltpu.VMEM((R, 128), F32),
            pltpu.VMEM((256, 128), F32),
            slices(NJ), slices(NJ), slices(NJ),
            slices(NI), slices(NI), slices(NI),
            slices(NI), slices(NJ),
            pltpu.VMEM((NI, K, 128), F32),
            pltpu.VMEM((NJ, K, 128), F32),
            dma(2 * K), dma(2),
            dma(NJ), dma(NJ), dma(NJ), dma(NJ),
            dma(NI), dma(NI), dma(NI), dma(NI),
            dma(NI), dma(NI), dma(NJ), dma(NJ),
            dma(NI), dma(NI), dma(NJ), dma(NJ),
        ],
        compiler_params=pltpu.CompilerParams(
            collective_id=0, has_side_effects=True, vmem_limit_bytes=48 * 1024 * 1024
        ),
    )(tensor, b_init.T, c_init)
    return a, b.T, c


def solution(mesh):
    in_specs = (P(None, "ia", "ja"), P("ja", None), P())
    out_specs = (P(("ia", "ja"), None), P("ja", None), P())
    return jax.shard_map(body, mesh=mesh, in_specs=in_specs, out_specs=out_specs, check_vma=False)
```
